32 devices in a mesh: dp: 8 (over y, x, core), tensor: 4 (over z).
Axes of the slice: x: 2, y: 2, z: 4, core: 2. Of those that a mesh axis runs over, the one named last changes fastest.
Arguments:
- tokens: bfloat16 [4096, 896], P(('dp', 'tensor')), parts along dimension 0, may hold values from -6 to 6
- smooth_scale: float32 [896], replicated, may hold values from 0.25 to 4
- gate_weight: bfloat16 [4864, 896], P('tensor'), may hold values from -0.1875 to 0.1875
- up_weight: bfloat16 [4864, 896], P('tensor'), may hold values from -0.1875 to 0.1875
- down_weight: bfloat16 [4864, 896], P('tensor'), may hold values from -0.078125 to 0.078125
Outputs:
- mixed: bfloat16 [4096, 896], P(('dp', 'tensor')), parts along dimension 0
The draws below stay inside these ranges and needn't reach their ends.
There are 8 independent parts, one for each index of `dp`. The reference program is written for one: setup_inputs(seed, part) draws one part's arguments, and reference() takes and returns one part's arrays. A program takes and returns all parts, laid end to end along the dimension named above; an argument that names none is the same for every part. Nothing has to cross between parts.
All inputs are finite; a program needn't handle non-finite values.
Results may differ from the reference program's by a relative error of at most 0.0064.
Values may be sent and summed in bfloat16 or wider, within the bound.
No kernel may reach another device: no remote copies, remote signals or barrier semaphores. Data moves between devices by JAX's collectives and lax.ppermute only.
A program may use at most 64 MiB of HBM per device.

```python
import math
import jax
import jax.numpy as jnp

D = 896
FF = 4864
TOKENS = 512


def shard_levels(rng, dims, pieces, low, largest):
    factor_of, own = 1.0, jax.random.fold_in(rng, 6)
    for dim, parts in pieces:
        draws = jnp.exp(jax.random.uniform(jax.random.fold_in(own, dim), (parts,), jnp.float32, low / len(pieces), largest / len(pieces)))
        factor_of = factor_of * jnp.repeat(draws, dims[dim] // parts).reshape([-1 if axis == dim else 1 for axis in range(len(dims))])
    return factor_of


def gaussian(key, extent, spread, most, split=(), dtype=jnp.bfloat16):
    array = spread * jax.random.normal(key, extent, jnp.float32)
    if split:
        array = array * shard_levels(key, extent, split, -0.22, 0.18)
    return jnp.clip(array, -most, most).astype(dtype)


def setup_inputs(seed: int = 0, part: int = 0) -> dict:
    seeds = jax.random.split(jax.random.key(seed), 6)
    own_keys = jax.random.split(jax.random.fold_in(seeds[5], part), 6)
    return {
        "tokens": gaussian(own_keys[0], (TOKENS, D), 1.0, 6.0, ((0, 4),)),
        "smooth_scale": jnp.clip(jnp.exp(jax.random.uniform(seeds[1], (D,), jnp.float32, math.log(0.25), math.log(4.0))), 0.25, 4.0),
        "gate_weight": gaussian(seeds[2], (FF, D), D ** -0.5, 0.1875, ((0, 4),)),
        "up_weight": gaussian(seeds[3], (FF, D), D ** -0.5, 0.1875, ((0, 4),)),
        "down_weight": gaussian(seeds[4], (FF, D), FF ** -0.5, 0.078125, ((0, 4),)),
    }


def reference(tokens, smooth_scale, gate_weight, up_weight, down_weight):
    smoothed = (tokens.astype(jnp.float32) / smooth_scale[None, :]).astype(jnp.bfloat16)
    gate_out = jnp.dot(smoothed, gate_weight.T, preferred_element_type=jnp.float32)
    up_out = jnp.dot(smoothed, up_weight.T, preferred_element_type=jnp.float32)
    hidden = (jax.nn.silu(gate_out) * up_out).astype(jnp.bfloat16)
    mixed = jnp.dot(hidden, down_weight, preferred_element_type=jnp.float32)
    return mixed.astype(jnp.bfloat16)
```

```python
import functools

import jax
import jax.numpy as jnp
from jax import lax
from jax.experimental import pallas as pl
from jax.experimental.pallas import tpu as pltpu
from jax.sharding import PartitionSpec as P

UNIT_TILE = 256
CONTRACT_LAST = (((1,), (1,)), ((), ()))
VMEM_LIMIT = 16 * 2**20
OWN_VMEM_LIMIT = 46 * 2**20
VMEM_SPEC = pl.BlockSpec(memory_space=pltpu.VMEM)
HBM_SPEC = pl.BlockSpec(memory_space=pltpu.HBM)


def unit_tiles(units):
    return [pl.ds(start, min(UNIT_TILE, units - start)) for start in range(0, units, UNIT_TILE)]


def hidden_tile(x, gate, up):
    gate_out = lax.dot_general(x, gate, CONTRACT_LAST, preferred_element_type=jnp.float32)
    up_out = lax.dot_general(x, up, CONTRACT_LAST, preferred_element_type=jnp.float32)
    return (gate_out / (1.0 + jnp.exp(-gate_out)) * up_out).astype(jnp.bfloat16)


def smooth(x, scale):
    return (x.astype(jnp.float32) / scale).astype(jnp.bfloat16)


def own_kernel(x_ref, scale_ref, gate_hbm, up_hbm, down_hbm, out_ref, gate_ref, up_ref, down_ref, hidden, sems):
    tiles = unit_tiles(gate_hbm.shape[0])
    copies = [
        [
            pltpu.make_async_copy(source.at[tile, :], target.at[tile, :], sems.at[which, index])
            for which, (source, target) in enumerate(((gate_hbm, gate_ref), (up_hbm, up_ref)))
        ]
        for index, tile in enumerate(tiles)
    ]
    down_copy = pltpu.make_async_copy(down_hbm, down_ref, sems.at[2, 0])
    for pair in copies:
        for copy in pair:
            copy.start()
    down_copy.start()
    x = smooth(x_ref[...], scale_ref[...])
    for pair, tile in zip(copies, tiles):
        for copy in pair:
            copy.wait()
        hidden[:, tile] = hidden_tile(x, gate_ref[tile, :], up_ref[tile, :])
    down_copy.wait()
    out_ref[...] = jnp.dot(hidden[...], down_ref[...], preferred_element_type=jnp.float32)


def arrived_kernel(x_ref, scale_ref, gate_ref, up_ref, down_ref, out_ref, hidden):
    x = smooth(x_ref[...], scale_ref[...])
    for tile in unit_tiles(gate_ref.shape[0]):
        hidden[:, tile] = hidden_tile(x, gate_ref[tile, :], up_ref[tile, :])
    out_ref[...] = jnp.dot(hidden[...], down_ref[...], preferred_element_type=jnp.float32).astype(out_ref.dtype)


def cost(rows, width, units):
    return pl.CostEstimate(flops=6 * rows * width * units, bytes_accessed=6 * units * width, transcendentals=2 * rows * units)


def own_block(x, scale, weights):
    rows, width = x.shape
    units = weights[0].shape[0]
    held = tuple(jax.ShapeDtypeStruct(w.shape, w.dtype) for w in weights)
    part, *kept = pl.pallas_call(
        own_kernel,
        out_shape=(jax.ShapeDtypeStruct((rows, width), jnp.float32),) + held,
        in_specs=[VMEM_SPEC] * 2 + [HBM_SPEC] * 3,
        out_specs=(VMEM_SPEC,) * 4,
        scratch_shapes=[pltpu.VMEM((rows, units), jnp.bfloat16), pltpu.SemaphoreType.DMA((3, len(unit_tiles(units))))],
        compiler_params=pltpu.CompilerParams(vmem_limit_bytes=OWN_VMEM_LIMIT),
        cost_estimate=cost(rows, width, units),
        name="own_block",
    )(x, scale, *weights)
    return part, kept


def arrived_block(x, scale, weights, dtype):
    rows, width = x.shape
    units = weights[0].shape[0]
    return pl.pallas_call(
        arrived_kernel,
        out_shape=jax.ShapeDtypeStruct((rows, width), dtype),
        in_specs=[VMEM_SPEC] * 5,
        out_specs=VMEM_SPEC,
        scratch_shapes=[pltpu.VMEM((rows, units), jnp.bfloat16)],
        compiler_params=pltpu.CompilerParams(vmem_limit_bytes=VMEM_LIMIT),
        cost_estimate=cost(rows, width, units),
        name="arrived_block",
    )(x, scale, *weights)


def shards(tokens, smooth_scale, gate_weight, up_weight, down_weight):
    n = lax.axis_size("tensor")
    ring = list(range(0, n, 2)) + list(range(1, n, 2))[::-1]
    route = [(ring[k - 1], ring[k]) for k in range(n)]
    send = functools.partial(lax.ppermute, axis_name="tensor", perm=route)
    scale = smooth_scale[None, :]
    own, weights = own_block(tokens, scale, (gate_weight, up_weight, down_weight))
    x, summed = tokens, None
    for hop in range(1, n):
        x = send(x)
        if hop == 1:
            summed = arrived_block(x, scale, weights, jnp.bfloat16)
        else:
            part = arrived_block(x, scale, weights, jnp.float32)
            summed = (send(summed).astype(jnp.float32) + part).astype(jnp.bfloat16)
    if n > 1:
        own = own + send(summed).astype(jnp.float32)
    return own.astype(jnp.bfloat16)


def solution(mesh):
    return jax.shard_map(
        shards,
        mesh=mesh,
        in_specs=(
            P(("dp", "tensor"), None),
            P(),
            P("tensor", None),
            P("tensor", None),
            P("tensor", None),
        ),
        out_specs=P(("dp", "tensor"), None),
        check_vma=False,
    )
```

```python
import jax
import jax.numpy as jnp
from jax import lax
from jax.experimental import pallas as pl
from jax.experimental.pallas import tpu as pltpu
from jax.sharding import PartitionSpec as P

UNIT_TILE = 256
CONTRACT_LAST = (((1,), (1,)), ((), ()))
VMEM_LIMIT = 16 * 2**20
OWN_VMEM_LIMIT = 46 * 2**20
VMEM_SPEC = pl.BlockSpec(memory_space=pltpu.VMEM)
HBM_SPEC = pl.BlockSpec(memory_space=pltpu.HBM)


def unit_tiles(units):
    return [pl.ds(start, min(UNIT_TILE, units - start)) for start in range(0, units, UNIT_TILE)]


def hidden_tile(x, gate, up):
    gate_out = lax.dot_general(x, gate, CONTRACT_LAST, preferred_element_type=jnp.float32)
    up_out = lax.dot_general(x, up, CONTRACT_LAST, preferred_element_type=jnp.float32)
    return (gate_out / (1.0 + jnp.exp(-gate_out)) * up_out).astype(jnp.bfloat16)


def smooth(x, scale):
    return (x.astype(jnp.float32) / scale).astype(jnp.bfloat16)


def own_kernel(x_ref, scale_ref, gate_hbm, up_hbm, down_hbm, out_ref, gate_ref, up_ref, down_ref, hidden, sems):
    tiles = unit_tiles(gate_hbm.shape[0])
    copies = [
        [
            pltpu.make_async_copy(source.at[tile, :], target.at[tile, :], sems.at[which, index])
            for which, (source, target) in enumerate(((gate_hbm, gate_ref), (up_hbm, up_ref)))
        ]
        for index, tile in enumerate(tiles)
    ]
    down_copy = pltpu.make_async_copy(down_hbm, down_ref, sems.at[2, 0])
    for pair in copies:
        for copy in pair:
            copy.start()
    down_copy.start()
    x = smooth(x_ref[...], scale_ref[...])
    for pair, tile in zip(copies, tiles):
        for copy in pair:
            copy.wait()
        hidden[:, tile] = hidden_tile(x, gate_ref[tile, :], up_ref[tile, :])
    down_copy.wait()
    out_ref[...] = jnp.dot(hidden[...], down_ref[...], preferred_element_type=jnp.float32)


def arrived_kernel(x_ref, scale_ref, gate_ref, up_ref, down_ref, out_ref, hidden):
    x = smooth(x_ref[...], scale_ref[...])
    for tile in unit_tiles(gate_ref.shape[0]):
        hidden[:, tile] = hidden_tile(x, gate_ref[tile, :], up_ref[tile, :])
    out_ref[...] = jnp.dot(hidden[...], down_ref[...], preferred_element_type=jnp.float32).astype(out_ref.dtype)


def cost(rows, width, units):
    return pl.CostEstimate(flops=6 * rows * width * units, bytes_accessed=6 * units * width, transcendentals=2 * rows * units)


def own_block(x, scale, weights):
    rows, width = x.shape
    units = weights[0].shape[0]
    held = tuple(jax.ShapeDtypeStruct(w.shape, w.dtype) for w in weights)
    part, *kept = pl.pallas_call(
        own_kernel,
        out_shape=(jax.ShapeDtypeStruct((rows, width), jnp.float32),) + held,
        in_specs=[VMEM_SPEC] * 2 + [HBM_SPEC] * 3,
        out_specs=(VMEM_SPEC,) * 4,
        scratch_shapes=[pltpu.VMEM((rows, units), jnp.bfloat16), pltpu.SemaphoreType.DMA((3, len(unit_tiles(units))))],
        compiler_params=pltpu.CompilerParams(vmem_limit_bytes=OWN_VMEM_LIMIT),
        cost_estimate=cost(rows, width, units),
        name="own_block",
    )(x, scale, *weights)
    return part, kept


def arrived_block(x, scale, weights, dtype):
    rows, width = x.shape
    units = weights[0].shape[0]
    return pl.pallas_call(
        arrived_kernel,
        out_shape=jax.ShapeDtypeStruct((rows, width), dtype),
        in_specs=[VMEM_SPEC] * 5,
        out_specs=VMEM_SPEC,
        scratch_shapes=[pltpu.VMEM((rows, units), jnp.bfloat16)],
        compiler_params=pltpu.CompilerParams(vmem_limit_bytes=VMEM_LIMIT),
        cost_estimate=cost(rows, width, units),
        name="arrived_block",
    )(x, scale, *weights)


def hop(block, route):
    return lax.ppermute(block, "tensor", route)


def add(arrived, part):
    return (arrived.astype(jnp.float32) + part).astype(jnp.bfloat16)


def line_of_four(tokens, own, scale, weights):
    across = {distance: [(place, place ^ distance) for place in range(4)] for distance in (1, 2, 3)}
    x_1 = hop(tokens, across[1])
    x_3, own = lax.optimization_barrier((hop(tokens, across[3]), own))
    part_1 = arrived_block(x_1, scale, weights, jnp.bfloat16)
    x_2 = hop(x_3, across[1])
    beside = hop(arrived_block(x_3, scale, weights, jnp.bfloat16), across[1])
    part_2, part_1 = lax.optimization_barrier((arrived_block(x_2, scale, weights, jnp.float32), part_1))
    from_neighbour = hop(part_1, across[1])
    from_far = hop(add(beside, part_2), across[2])
    return (own + from_neighbour.astype(jnp.float32) + from_far.astype(jnp.float32)).astype(jnp.bfloat16)


def folded_ring(tokens, own, scale, weights, n):
    order = list(range(0, n, 2)) + list(range(1, n, 2))[::-1]
    route = [(order[k - 1], order[k]) for k in range(n)]
    x, summed = tokens, None
    for step in range(1, n):
        x = hop(x, route)
        part = arrived_block(x, scale, weights, jnp.bfloat16 if step == 1 else jnp.float32)
        summed = part if step == 1 else add(hop(summed, route), part)
    return add(hop(summed, route), own) if n > 1 else own.astype(jnp.bfloat16)


def shards(tokens, smooth_scale, gate_weight, up_weight, down_weight):
    n = lax.axis_size("tensor")
    scale = smooth_scale[None, :]
    own, weights = own_block(tokens, scale, (gate_weight, up_weight, down_weight))
    if n == 4:
        return line_of_four(tokens, own, scale, weights)
    return folded_ring(tokens, own, scale, weights, n)


def solution(mesh):
    return jax.shard_map(
        shards,
        mesh=mesh,
        in_specs=(
            P(("dp", "tensor"), None),
            P(),
            P("tensor", None),
            P("tensor", None),
            P("tensor", None),
        ),
        out_specs=P(("dp", "tensor"), None),
        check_vma=False,
    )
```

```python
import jax
import jax.numpy as jnp
from jax import lax
from jax.experimental import pallas as pl
from jax.experimental.pallas import tpu as pltpu
from jax.sharding import PartitionSpec as P

UNIT_TILE = 256
CONTRACT_LAST = (((1,), (1,)), ((), ()))
VMEM_LIMIT = 16 * 2**20
OWN_VMEM_LIMIT = 46 * 2**20
VMEM_SPEC = pl.BlockSpec(memory_space=pltpu.VMEM)
HBM_SPEC = pl.BlockSpec(memory_space=pltpu.HBM)


def unit_tiles(units):
    return [pl.ds(start, min(UNIT_TILE, units - start)) for start in range(0, units, UNIT_TILE)]


def hidden_tile(x, gate, up):
    gate_out = lax.dot_general(x, gate, CONTRACT_LAST, preferred_element_type=jnp.float32)
    up_out = lax.dot_general(x, up, CONTRACT_LAST, preferred_element_type=jnp.float32)
    return (gate_out / (1.0 + jnp.exp(-gate_out)) * up_out).astype(jnp.bfloat16)


def smooth(x, scale):
    return (x.astype(jnp.float32) / scale).astype(jnp.bfloat16)


def own_kernel(x_ref, scale_ref, gate_hbm, up_hbm, down_hbm, out_ref, gate_ref, up_ref, down_ref, hidden, sems):
    tiles = unit_tiles(gate_hbm.shape[0])
    copies = [
        [
            pltpu.make_async_copy(source.at[tile, :], target.at[tile, :], sems.at[which, index])
            for which, (source, target) in enumerate(((gate_hbm, gate_ref), (up_hbm, up_ref)))
        ]
        for index, tile in enumerate(tiles)
    ]
    down_copy = pltpu.make_async_copy(down_hbm, down_ref, sems.at[2, 0])
    for pair in copies:
        for copy in pair:
            copy.start()
    down_copy.start()
    x = smooth(x_ref[...], scale_ref[...])
    for pair, tile in zip(copies, tiles):
        for copy in pair:
            copy.wait()
        hidden[:, tile] = hidden_tile(x, gate_ref[tile, :], up_ref[tile, :])
    down_copy.wait()
    out_ref[...] = jnp.dot(hidden[...], down_ref[...], preferred_element_type=jnp.float32)


def arrived_kernel(x_ref, scale_ref, gate_ref, up_ref, down_ref, out_ref, hidden):
    x = smooth(x_ref[...], scale_ref[...])
    for tile in unit_tiles(gate_ref.shape[0]):
        hidden[:, tile] = hidden_tile(x, gate_ref[tile, :], up_ref[tile, :])
    out_ref[...] = jnp.dot(hidden[...], down_ref[...], preferred_element_type=jnp.float32).astype(out_ref.dtype)


def cost(rows, width, units):
    return pl.CostEstimate(flops=6 * rows * width * units, bytes_accessed=6 * units * width, transcendentals=2 * rows * units)


def own_block(x, scale, weights):
    rows, width = x.shape
    units = weights[0].shape[0]
    held = tuple(jax.ShapeDtypeStruct(w.shape, w.dtype) for w in weights)
    part, *kept = pl.pallas_call(
        own_kernel,
        out_shape=(jax.ShapeDtypeStruct((rows, width), jnp.float32),) + held,
        in_specs=[VMEM_SPEC] * 2 + [HBM_SPEC] * 3,
        out_specs=(VMEM_SPEC,) * 4,
        scratch_shapes=[pltpu.VMEM((rows, units), jnp.bfloat16), pltpu.SemaphoreType.DMA((3, len(unit_tiles(units))))],
        compiler_params=pltpu.CompilerParams(vmem_limit_bytes=OWN_VMEM_LIMIT),
        cost_estimate=cost(rows, width, units),
        name="own_block",
    )(x, scale, *weights)
    return part, kept


def arrived_block(x, scale, weights, dtype):
    rows, width = x.shape
    units = weights[0].shape[0]
    return pl.pallas_call(
        arrived_kernel,
        out_shape=jax.ShapeDtypeStruct((rows, width), dtype),
        in_specs=[VMEM_SPEC] * 5,
        out_specs=VMEM_SPEC,
        scratch_shapes=[pltpu.VMEM((rows, units), jnp.bfloat16)],
        compiler_params=pltpu.CompilerParams(vmem_limit_bytes=VMEM_LIMIT),
        cost_estimate=cost(rows, width, units),
        name="arrived_block",
    )(x, scale, *weights)


def hop(block, route):
    return lax.ppermute(block, "tensor", route)


def add(arrived, part):
    return (arrived.astype(jnp.float32) + part).astype(jnp.bfloat16)


def line_of_four(tokens, own, scale, weights):
    across = {distance: [(place, place ^ distance) for place in range(4)] for distance in (1, 2, 3)}
    x_1 = hop(tokens, across[1])
    x_3, own = lax.optimization_barrier((hop(tokens, across[3]), own))
    part_1 = arrived_block(x_1, scale, weights, jnp.bfloat16)
    x_2 = hop(x_3, across[1])
    beside = hop(arrived_block(x_3, scale, weights, jnp.bfloat16), across[1])
    from_neighbour = hop(part_1, across[1])
    part_2 = arrived_block(x_2, scale, weights, jnp.float32)
    from_far = hop(add(beside, part_2), across[2])
    return (own + from_neighbour.astype(jnp.float32) + from_far.astype(jnp.float32)).astype(jnp.bfloat16)


def folded_ring(tokens, own, scale, weights, n):
    order = list(range(0, n, 2)) + list(range(1, n, 2))[::-1]
    route = [(order[k - 1], order[k]) for k in range(n)]
    x, summed = tokens, None
    for step in range(1, n):
        x = hop(x, route)
        part = arrived_block(x, scale, weights, jnp.bfloat16 if step == 1 else jnp.float32)
        summed = part if step == 1 else add(hop(summed, route), part)
    return add(hop(summed, route), own) if n > 1 else own.astype(jnp.bfloat16)


def shards(tokens, smooth_scale, gate_weight, up_weight, down_weight):
    n = lax.axis_size("tensor")
    scale = smooth_scale[None, :]
    own, weights = own_block(tokens, scale, (gate_weight, up_weight, down_weight))
    if n == 4:
        return line_of_four(tokens, own, scale, weights)
    return folded_ring(tokens, own, scale, weights, n)


def solution(mesh):
    return jax.shard_map(
        shards,
        mesh=mesh,
        in_specs=(
            P(("dp", "tensor"), None),
            P(),
            P("tensor", None),
            P("tensor", None),
            P("tensor", None),
        ),
        out_specs=P(("dp", "tensor"), None),
        check_vma=False,
    )
```

```python
import jax
import jax.numpy as jnp
from jax import lax
from jax.experimental import pallas as pl
from jax.experimental.pallas import tpu as pltpu
from jax.sharding import PartitionSpec as P

UNIT_TILE = 256
CONTRACT_LAST = (((1,), (1,)), ((), ()))
VMEM_LIMIT = 16 * 2**20
OWN_VMEM_LIMIT = 46 * 2**20
VMEM_SPEC = pl.BlockSpec(memory_space=pltpu.VMEM)
HBM_SPEC = pl.BlockSpec(memory_space=pltpu.HBM)


def unit_tiles(units):
    return [pl.ds(start, min(UNIT_TILE, units - start)) for start in range(0, units, UNIT_TILE)]


def hidden_tile(x, gate, up):
    gate_out = lax.dot_general(x, gate, CONTRACT_LAST, preferred_element_type=jnp.float32)
    up_out = lax.dot_general(x, up, CONTRACT_LAST, preferred_element_type=jnp.float32)
    return (gate_out / (1.0 + jnp.exp(-gate_out)) * up_out).astype(jnp.bfloat16)


def smooth(x, scale):
    return (x.astype(jnp.float32) / scale).astype(jnp.bfloat16)


def own_kernel(x_ref, scale_ref, gate_hbm, up_hbm, down_hbm, out_ref, gate_ref, up_ref, down_ref, hidden, sems):
    tiles = unit_tiles(gate_hbm.shape[0])
    copies = [
        [
            pltpu.make_async_copy(source.at[tile, :], target.at[tile, :], sems.at[which, index])
            for which, (source, target) in enumerate(((gate_hbm, gate_ref), (up_hbm, up_ref)))
        ]
        for index, tile in enumerate(tiles)
    ]
    down_copy = pltpu.make_async_copy(down_hbm, down_ref, sems.at[2, 0])
    for pair in copies:
        for copy in pair:
            copy.start()
    down_copy.start()
    x = smooth(x_ref[...], scale_ref[...])
    for pair, tile in zip(copies, tiles):
        for copy in pair:
            copy.wait()
        hidden[:, tile] = hidden_tile(x, gate_ref[tile, :], up_ref[tile, :])
    down_copy.wait()
    out_ref[...] = jnp.dot(hidden[...], down_ref[...], preferred_element_type=jnp.float32)


def arrived_kernel(x_ref, scale_ref, gate_ref, up_ref, down_ref, out_ref, hidden):
    x = smooth(x_ref[...], scale_ref[...])
    for tile in unit_tiles(gate_ref.shape[0]):
        hidden[:, tile] = hidden_tile(x, gate_ref[tile, :], up_ref[tile, :])
    out_ref[...] = jnp.dot(hidden[...], down_ref[...], preferred_element_type=jnp.float32).astype(out_ref.dtype)


def cost(rows, width, units):
    return pl.CostEstimate(flops=6 * rows * width * units, bytes_accessed=6 * units * width, transcendentals=2 * rows * units)


def own_block(x, scale, weights):
    rows, width = x.shape
    units = weights[0].shape[0]
    held = tuple(jax.ShapeDtypeStruct(w.shape, w.dtype) for w in weights)
    part, *kept = pl.pallas_call(
        own_kernel,
        out_shape=(jax.ShapeDtypeStruct((rows, width), jnp.float32),) + held,
        in_specs=[VMEM_SPEC] * 2 + [HBM_SPEC] * 3,
        out_specs=(VMEM_SPEC,) * 4,
        scratch_shapes=[pltpu.VMEM((rows, units), jnp.bfloat16), pltpu.SemaphoreType.DMA((3, len(unit_tiles(units))))],
        compiler_params=pltpu.CompilerParams(vmem_limit_bytes=OWN_VMEM_LIMIT),
        cost_estimate=cost(rows, width, units),
        name="own_block",
    )(x, scale, *weights)
    return part, kept


def arrived_block(x, scale, weights, dtype):
    rows, width = x.shape
    units = weights[0].shape[0]
    return pl.pallas_call(
        arrived_kernel,
        out_shape=jax.ShapeDtypeStruct((rows, width), dtype),
        in_specs=[VMEM_SPEC] * 5,
        out_specs=VMEM_SPEC,
        scratch_shapes=[pltpu.VMEM((rows, units), jnp.bfloat16)],
        compiler_params=pltpu.CompilerParams(vmem_limit_bytes=VMEM_LIMIT),
        cost_estimate=cost(rows, width, units),
        name="arrived_block",
    )(x, scale, *weights)


def hop(block, route):
    return lax.ppermute(block, "tensor", route)


def add(arrived, part):
    return (arrived.astype(jnp.float32) + part).astype(jnp.bfloat16)


def line_of_four(tokens, own, scale, weights):
    across = {distance: [(place, place ^ distance) for place in range(4)] for distance in (1, 2, 3)}
    x_1 = hop(tokens, across[1])
    x_2, own = lax.optimization_barrier((hop(tokens, across[2]), own))
    part_1 = arrived_block(x_1, scale, weights, jnp.bfloat16)
    x_3 = hop(x_2, across[1])
    beside = hop(arrived_block(x_2, scale, weights, jnp.bfloat16), across[1])
    from_neighbour = hop(part_1, across[1])
    part_3 = arrived_block(x_3, scale, weights, jnp.float32)
    from_far = hop(add(beside, part_3), across[3])
    return (own + from_neighbour.astype(jnp.float32) + from_far.astype(jnp.float32)).astype(jnp.bfloat16)


def folded_ring(tokens, own, scale, weights, n):
    order = list(range(0, n, 2)) + list(range(1, n, 2))[::-1]
    route = [(order[k - 1], order[k]) for k in range(n)]
    x, summed = tokens, None
    for step in range(1, n):
        x = hop(x, route)
        part = arrived_block(x, scale, weights, jnp.bfloat16 if step == 1 else jnp.float32)
        summed = part if step == 1 else add(hop(summed, route), part)
    return add(hop(summed, route), own) if n > 1 else own.astype(jnp.bfloat16)


def shards(tokens, smooth_scale, gate_weight, up_weight, down_weight):
    n = lax.axis_size("tensor")
    scale = smooth_scale[None, :]
    own, weights = own_block(tokens, scale, (gate_weight, up_weight, down_weight))
    if n == 4:
        return line_of_four(tokens, own, scale, weights)
    return folded_ring(tokens, own, scale, weights, n)


def solution(mesh):
    return jax.shard_map(
        shards,
        mesh=mesh,
        in_specs=(
            P(("dp", "tensor"), None),
            P(),
            P("tensor", None),
            P("tensor", None),
            P("tensor", None),
        ),
        out_specs=P(("dp", "tensor"), None),
        check_vma=False,
    )
```

```python
import jax
import jax.numpy as jnp
from jax import lax
from jax.experimental import pallas as pl
from jax.experimental.pallas import tpu as pltpu
from jax.sharding import PartitionSpec as P

UNIT_TILE = 256
CONTRACT_LAST = (((1,), (1,)), ((), ()))
VMEM_LIMIT = 16 * 2**20
OWN_VMEM_LIMIT = 46 * 2**20
VMEM_SPEC = pl.BlockSpec(memory_space=pltpu.VMEM)
HBM_SPEC = pl.BlockSpec(memory_space=pltpu.HBM)


def unit_tiles(units):
    return [pl.ds(start, min(UNIT_TILE, units - start)) for start in range(0, units, UNIT_TILE)]


def hidden_tile(x, gate, up):
    gate_out = lax.dot_general(x, gate, CONTRACT_LAST, preferred_element_type=jnp.float32)
    up_out = lax.dot_general(x, up, CONTRACT_LAST, preferred_element_type=jnp.float32)
    return (gate_out / (1.0 + jnp.exp(-gate_out)) * up_out).astype(jnp.bfloat16)


def smooth(x, scale):
    return (x.astype(jnp.float32) / scale).astype(jnp.bfloat16)


def own_kernel(x_ref, scale_ref, gate_hbm, up_hbm, down_hbm, out_ref, gate_ref, up_ref, down_ref, hidden, sems):
    tiles = unit_tiles(gate_hbm.shape[0])
    copies = [
        [
            pltpu.make_async_copy(source.at[tile, :], target.at[tile, :], sems.at[which, index])
            for which, (source, target) in enumerate(((gate_hbm, gate_ref), (up_hbm, up_ref)))
        ]
        for index, tile in enumerate(tiles)
    ]
    down_copy = pltpu.make_async_copy(down_hbm, down_ref, sems.at[2, 0])
    for pair in copies:
        for copy in pair:
            copy.start()
    down_copy.start()
    x = smooth(x_ref[...], scale_ref[...])
    for pair, tile in zip(copies, tiles):
        for copy in pair:
            copy.wait()
        hidden[:, tile] = hidden_tile(x, gate_ref[tile, :], up_ref[tile, :])
    down_copy.wait()
    out_ref[...] = jnp.dot(hidden[...], down_ref[...], preferred_element_type=jnp.float32)


def arrived_kernel(x_ref, scale_ref, gate_ref, up_ref, down_ref, out_ref, hidden):
    x = smooth(x_ref[...], scale_ref[...])
    for tile in unit_tiles(gate_ref.shape[0]):
        hidden[:, tile] = hidden_tile(x, gate_ref[tile, :], up_ref[tile, :])
    out_ref[...] = jnp.dot(hidden[...], down_ref[...], preferred_element_type=jnp.float32).astype(out_ref.dtype)


def cost(rows, width, units):
    return pl.CostEstimate(flops=6 * rows * width * units, bytes_accessed=6 * units * width, transcendentals=2 * rows * units)


def own_block(x, scale, weights):
    rows, width = x.shape
    units = weights[0].shape[0]
    held = tuple(jax.ShapeDtypeStruct(w.shape, w.dtype) for w in weights)
    part, *kept = pl.pallas_call(
        own_kernel,
        out_shape=(jax.ShapeDtypeStruct((rows, width), jnp.float32),) + held,
        in_specs=[VMEM_SPEC] * 2 + [HBM_SPEC] * 3,
        out_specs=(VMEM_SPEC,) * 4,
        scratch_shapes=[pltpu.VMEM((rows, units), jnp.bfloat16), pltpu.SemaphoreType.DMA((3, len(unit_tiles(units))))],
        compiler_params=pltpu.CompilerParams(vmem_limit_bytes=OWN_VMEM_LIMIT),
        cost_estimate=cost(rows, width, units),
        name="own_block",
    )(x, scale, *weights)
    return part, kept


def arrived_block(x, scale, weights, dtype):
    rows, width = x.shape
    units = weights[0].shape[0]
    return pl.pallas_call(
        arrived_kernel,
        out_shape=jax.ShapeDtypeStruct((rows, width), dtype),
        in_specs=[VMEM_SPEC] * 5,
        out_specs=VMEM_SPEC,
        scratch_shapes=[pltpu.VMEM((rows, units), jnp.bfloat16)],
        compiler_params=pltpu.CompilerParams(vmem_limit_bytes=VMEM_LIMIT),
        cost_estimate=cost(rows, width, units),
        name="arrived_block",
    )(x, scale, *weights)


def hop(block, route):
    return lax.ppermute(block, "tensor", route)


def add(arrived, part):
    return (arrived.astype(jnp.float32) + part).astype(jnp.bfloat16)


def line_of_four(tokens, own, scale, weights):
    across = {distance: [(place, place ^ distance) for place in range(4)] for distance in (1, 2, 3)}
    x_1 = hop(tokens, across[1])
    x_3, own = lax.optimization_barrier((hop(tokens, across[3]), own))
    x_2 = hop(x_3, across[1])
    own = own.astype(jnp.float32)
    for x, distance in ((x_3, 3), (x_1, 1), (x_2, 2)):
        own = own + hop(arrived_block(x, scale, weights, jnp.bfloat16), across[distance]).astype(jnp.float32)
    return own.astype(jnp.bfloat16)


def folded_ring(tokens, own, scale, weights, n):
    order = list(range(0, n, 2)) + list(range(1, n, 2))[::-1]
    route = [(order[k - 1], order[k]) for k in range(n)]
    x, summed = tokens, None
    for step in range(1, n):
        x = hop(x, route)
        part = arrived_block(x, scale, weights, jnp.bfloat16 if step == 1 else jnp.float32)
        summed = part if step == 1 else add(hop(summed, route), part)
    return add(hop(summed, route), own) if n > 1 else own.astype(jnp.bfloat16)


def shards(tokens, smooth_scale, gate_weight, up_weight, down_weight):
    n = lax.axis_size("tensor")
    scale = smooth_scale[None, :]
    own, weights = own_block(tokens, scale, (gate_weight, up_weight, down_weight))
    if n == 4:
        return line_of_four(tokens, own, scale, weights)
    return folded_ring(tokens, own, scale, weights, n)


def solution(mesh):
    return jax.shard_map(
        shards,
        mesh=mesh,
        in_specs=(
            P(("dp", "tensor"), None),
            P(),
            P("tensor", None),
            P("tensor", None),
            P("tensor", None),
        ),
        out_specs=P(("dp", "tensor"), None),
        check_vma=False,
    )
```

```python
import jax
import jax.numpy as jnp
from jax import lax
from jax.experimental import pallas as pl
from jax.experimental.pallas import tpu as pltpu
from jax.sharding import PartitionSpec as P

UNIT_TILE = 256
CONTRACT_LAST = (((1,), (1,)), ((), ()))
VMEM_LIMIT = 16 * 2**20
OWN_VMEM_LIMIT = 46 * 2**20
VMEM_SPEC = pl.BlockSpec(memory_space=pltpu.VMEM)
HBM_SPEC = pl.BlockSpec(memory_space=pltpu.HBM)


def unit_tiles(units):
    return [pl.ds(start, min(UNIT_TILE, units - start)) for start in range(0, units, UNIT_TILE)]


def hidden_tile(x, gate, up):
    gate_out = lax.dot_general(x, gate, CONTRACT_LAST, preferred_element_type=jnp.float32)
    up_out = lax.dot_general(x, up, CONTRACT_LAST, preferred_element_type=jnp.float32)
    return (gate_out / (1.0 + jnp.exp(-gate_out)) * up_out).astype(jnp.bfloat16)


def smooth(x, scale):
    return (x.astype(jnp.float32) / scale).astype(jnp.bfloat16)


def own_kernel(x_ref, scale_ref, gate_hbm, up_hbm, down_hbm, out_ref, gate_ref, up_ref, down_ref, hidden, sems):
    tiles = unit_tiles(gate_hbm.shape[0])
    copies = [
        [
            pltpu.make_async_copy(source.at[tile, :], target.at[tile, :], sems.at[which, index])
            for which, (source, target) in enumerate(((gate_hbm, gate_ref), (up_hbm, up_ref)))
        ]
        for index, tile in enumerate(tiles)
    ]
    down_copy = pltpu.make_async_copy(down_hbm, down_ref, sems.at[2, 0])
    for pair in copies:
        for copy in pair:
            copy.start()
    down_copy.start()
    x = smooth(x_ref[...], scale_ref[...])
    for pair, tile in zip(copies, tiles):
        for copy in pair:
            copy.wait()
        hidden[:, tile] = hidden_tile(x, gate_ref[tile, :], up_ref[tile, :])
    down_copy.wait()
    out_ref[...] = jnp.dot(hidden[...], down_ref[...], preferred_element_type=jnp.float32)


def arrived_kernel(x_ref, scale_ref, gate_ref, up_ref, down_ref, out_ref, hidden):
    x = smooth(x_ref[...], scale_ref[...])
    for tile in unit_tiles(gate_ref.shape[0]):
        hidden[:, tile] = hidden_tile(x, gate_ref[tile, :], up_ref[tile, :])
    out_ref[...] = jnp.dot(hidden[...], down_ref[...], preferred_element_type=jnp.float32).astype(out_ref.dtype)


def cost(rows, width, units):
    return pl.CostEstimate(flops=6 * rows * width * units, bytes_accessed=6 * units * width, transcendentals=2 * rows * units)


def own_block(x, scale, weights):
    rows, width = x.shape
    units = weights[0].shape[0]
    held = tuple(jax.ShapeDtypeStruct(w.shape, w.dtype) for w in weights)
    part, *kept = pl.pallas_call(
        own_kernel,
        out_shape=(jax.ShapeDtypeStruct((rows, width), jnp.float32),) + held,
        in_specs=[VMEM_SPEC] * 2 + [HBM_SPEC] * 3,
        out_specs=(VMEM_SPEC,) * 4,
        scratch_shapes=[pltpu.VMEM((rows, units), jnp.bfloat16), pltpu.SemaphoreType.DMA((3, len(unit_tiles(units))))],
        compiler_params=pltpu.CompilerParams(vmem_limit_bytes=OWN_VMEM_LIMIT),
        cost_estimate=cost(rows, width, units),
        name="own_block",
    )(x, scale, *weights)
    return part, kept


def arrived_block(x, scale, weights, dtype):
    rows, width = x.shape
    units = weights[0].shape[0]
    return pl.pallas_call(
        arrived_kernel,
        out_shape=jax.ShapeDtypeStruct((rows, width), dtype),
        in_specs=[VMEM_SPEC] * 5,
        out_specs=VMEM_SPEC,
        scratch_shapes=[pltpu.VMEM((rows, units), jnp.bfloat16)],
        compiler_params=pltpu.CompilerParams(vmem_limit_bytes=VMEM_LIMIT),
        cost_estimate=cost(rows, width, units),
        name="arrived_block",
    )(x, scale, *weights)


def hop(block, route):
    return lax.ppermute(block, "tensor", route)


def add(arrived, part):
    return (arrived.astype(jnp.float32) + part).astype(jnp.bfloat16)


def line_of_four(tokens, own, scale, weights):
    across = {distance: [(place, place ^ distance) for place in range(4)] for distance in (1, 2, 3)}
    x_1 = hop(tokens, across[1])
    x_3, own = lax.optimization_barrier((hop(tokens, across[3]), own))
    x_2 = hop(x_3, across[1])
    from_mirror = hop(arrived_block(x_3, scale, weights, jnp.bfloat16), across[3])
    part_1 = arrived_block(x_1, scale, weights, jnp.bfloat16)
    part_2, part_1 = lax.optimization_barrier((arrived_block(x_2, scale, weights, jnp.bfloat16), part_1))
    for arrived in (from_mirror, hop(part_2, across[2]), hop(part_1, across[1])):
        own = own + arrived.astype(jnp.float32)
    return own.astype(jnp.bfloat16)


def folded_ring(tokens, own, scale, weights, n):
    order = list(range(0, n, 2)) + list(range(1, n, 2))[::-1]
    route = [(order[k - 1], order[k]) for k in range(n)]
    x, summed = tokens, None
    for step in range(1, n):
        x = hop(x, route)
        part = arrived_block(x, scale, weights, jnp.bfloat16 if step == 1 else jnp.float32)
        summed = part if step == 1 else add(hop(summed, route), part)
    return add(hop(summed, route), own) if n > 1 else own.astype(jnp.bfloat16)


def shards(tokens, smooth_scale, gate_weight, up_weight, down_weight):
    n = lax.axis_size("tensor")
    scale = smooth_scale[None, :]
    own, weights = own_block(tokens, scale, (gate_weight, up_weight, down_weight))
    if n == 4:
        return line_of_four(tokens, own, scale, weights)
    return folded_ring(tokens, own, scale, weights, n)


def solution(mesh):
    return jax.shard_map(
        shards,
        mesh=mesh,
        in_specs=(
            P(("dp", "tensor"), None),
            P(),
            P("tensor", None),
            P("tensor", None),
            P("tensor", None),
        ),
        out_specs=P(("dp", "tensor"), None),
        check_vma=False,
    )
```

```python
import jax
import jax.numpy as jnp
from jax import lax
from jax.experimental import pallas as pl
from jax.experimental.pallas import tpu as pltpu
from jax.sharding import PartitionSpec as P

UNIT_TILE = 256
CONTRACT_LAST = (((1,), (1,)), ((), ()))
VMEM_LIMIT = 16 * 2**20
OWN_VMEM_LIMIT = 46 * 2**20
VMEM_SPEC = pl.BlockSpec(memory_space=pltpu.VMEM)
HBM_SPEC = pl.BlockSpec(memory_space=pltpu.HBM)


def unit_tiles(units):
    return [pl.ds(start, min(UNIT_TILE, units - start)) for start in range(0, units, UNIT_TILE)]


def hidden_tile(x, gate, up):
    gate_out = lax.dot_general(x, gate, CONTRACT_LAST, preferred_element_type=jnp.float32)
    up_out = lax.dot_general(x, up, CONTRACT_LAST, preferred_element_type=jnp.float32)
    return (gate_out / (1.0 + jnp.exp(-gate_out)) * up_out).astype(jnp.bfloat16)


def smooth(x, scale):
    return (x.astype(jnp.float32) / scale).astype(jnp.bfloat16)


def own_kernel(x_ref, scale_ref, gate_hbm, up_hbm, down_hbm, out_ref, gate_ref, up_ref, down_ref, hidden, sems):
    tiles = unit_tiles(gate_hbm.shape[0])
    copies = [
        [
            pltpu.make_async_copy(source.at[tile, :], target.at[tile, :], sems.at[which, index])
            for which, (source, target) in enumerate(((gate_hbm, gate_ref), (up_hbm, up_ref)))
        ]
        for index, tile in enumerate(tiles)
    ]
    down_copy = pltpu.make_async_copy(down_hbm, down_ref, sems.at[2, 0])
    for pair in copies:
        for copy in pair:
            copy.start()
    down_copy.start()
    x = smooth(x_ref[...], scale_ref[...])
    for pair, tile in zip(copies, tiles):
        for copy in pair:
            copy.wait()
        hidden[:, tile] = hidden_tile(x, gate_ref[tile, :], up_ref[tile, :])
    down_copy.wait()
    out_ref[...] = jnp.dot(hidden[...], down_ref[...], preferred_element_type=jnp.float32)


def arrived_kernel(x_ref, scale_ref, gate_ref, up_ref, down_ref, out_ref, hidden):
    x = smooth(x_ref[...], scale_ref[...])
    for tile in unit_tiles(gate_ref.shape[0]):
        hidden[:, tile] = hidden_tile(x, gate_ref[tile, :], up_ref[tile, :])
    out_ref[...] = jnp.dot(hidden[...], down_ref[...], preferred_element_type=jnp.float32).astype(out_ref.dtype)


def cost(rows, width, units):
    return pl.CostEstimate(flops=6 * rows * width * units, bytes_accessed=6 * units * width, transcendentals=2 * rows * units)


def own_block(x, scale, weights):
    rows, width = x.shape
    units = weights[0].shape[0]
    held = tuple(jax.ShapeDtypeStruct(w.shape, w.dtype) for w in weights)
    part, *kept = pl.pallas_call(
        own_kernel,
        out_shape=(jax.ShapeDtypeStruct((rows, width), jnp.float32),) + held,
        in_specs=[VMEM_SPEC] * 2 + [HBM_SPEC] * 3,
        out_specs=(VMEM_SPEC,) * 4,
        scratch_shapes=[pltpu.VMEM((rows, units), jnp.bfloat16), pltpu.SemaphoreType.DMA((3, len(unit_tiles(units))))],
        compiler_params=pltpu.CompilerParams(vmem_limit_bytes=OWN_VMEM_LIMIT),
        cost_estimate=cost(rows, width, units),
        name="own_block",
    )(x, scale, *weights)
    return part, kept


def arrived_block(x, scale, weights, dtype):
    rows, width = x.shape
    units = weights[0].shape[0]
    return pl.pallas_call(
        arrived_kernel,
        out_shape=jax.ShapeDtypeStruct((rows, width), dtype),
        in_specs=[VMEM_SPEC] * 5,
        out_specs=VMEM_SPEC,
        scratch_shapes=[pltpu.VMEM((rows, units), jnp.bfloat16)],
        compiler_params=pltpu.CompilerParams(vmem_limit_bytes=VMEM_LIMIT),
        cost_estimate=cost(rows, width, units),
        name="arrived_block",
    )(x, scale, *weights)


def hop(block, route, axes="tensor"):
    return lax.ppermute(block, axes, route)


def add(arrived, part):
    return (arrived.astype(jnp.float32) + part).astype(jnp.bfloat16)


def line_of_four(tokens, own, scale, weights):
    beside = [(place, place ^ 1) for place in range(4)]
    groups = range(lax.axis_size("dp"))

    def far(distances):
        return [(group * 4 + place, group * 4 + (place ^ distances[group % 2])) for group in groups for place in range(4)]

    def far_hop(block, distances):
        return hop(block, far(distances), ("dp", "tensor"))

    x_1 = hop(tokens, beside)
    x_far, own = lax.optimization_barrier((far_hop(tokens, (2, 3)), own))
    part_1 = arrived_block(x_1, scale, weights, jnp.bfloat16)
    x_last = hop(x_far, beside)
    joining = hop(arrived_block(x_far, scale, weights, jnp.bfloat16), beside)
    from_neighbour = hop(part_1, beside)
    from_far = far_hop(add(joining, arrived_block(x_last, scale, weights, jnp.float32)), (3, 2))
    return (own + from_neighbour.astype(jnp.float32) + from_far.astype(jnp.float32)).astype(jnp.bfloat16)


def folded_ring(tokens, own, scale, weights, n):
    order = list(range(0, n, 2)) + list(range(1, n, 2))[::-1]
    route = [(order[k - 1], order[k]) for k in range(n)]
    x, summed = tokens, None
    for step in range(1, n):
        x = hop(x, route)
        part = arrived_block(x, scale, weights, jnp.bfloat16 if step == 1 else jnp.float32)
        summed = part if step == 1 else add(hop(summed, route), part)
    return add(hop(summed, route), own) if n > 1 else own.astype(jnp.bfloat16)


def shards(tokens, smooth_scale, gate_weight, up_weight, down_weight):
    n = lax.axis_size("tensor")
    scale = smooth_scale[None, :]
    own, weights = own_block(tokens, scale, (gate_weight, up_weight, down_weight))
    if n == 4:
        return line_of_four(tokens, own, scale, weights)
    return folded_ring(tokens, own, scale, weights, n)


def solution(mesh):
    return jax.shard_map(
        shards,
        mesh=mesh,
        in_specs=(
            P(("dp", "tensor"), None),
            P(),
            P("tensor", None),
            P("tensor", None),
            P("tensor", None),
        ),
        out_specs=P(("dp", "tensor"), None),
        check_vma=False,
    )
```

```python
import jax
import jax.numpy as jnp
from jax import lax
from jax.experimental import pallas as pl
from jax.experimental.pallas import tpu as pltpu
from jax.sharding import PartitionSpec as P

UNIT_TILE = 256
CONTRACT_LAST = (((1,), (1,)), ((), ()))
VMEM_LIMIT = 16 * 2**20
OWN_VMEM_LIMIT = 46 * 2**20
VMEM_SPEC = pl.BlockSpec(memory_space=pltpu.VMEM)
HBM_SPEC = pl.BlockSpec(memory_space=pltpu.HBM)


def unit_tiles(units):
    return [pl.ds(start, min(UNIT_TILE, units - start)) for start in range(0, units, UNIT_TILE)]


def hidden_tile(x, gate, up):
    gate_out = lax.dot_general(x, gate, CONTRACT_LAST, preferred_element_type=jnp.float32)
    up_out = lax.dot_general(x, up, CONTRACT_LAST, preferred_element_type=jnp.float32)
    return (gate_out / (1.0 + jnp.exp(-gate_out)) * up_out).astype(jnp.bfloat16)


def smooth(x, scale):
    return (x.astype(jnp.float32) / scale).astype(jnp.bfloat16)


def own_kernel(x_ref, scale_ref, gate_hbm, up_hbm, down_hbm, out_ref, gate_ref, up_ref, down_ref, hidden, sems):
    tiles = unit_tiles(gate_hbm.shape[0])
    copies = [
        [
            pltpu.make_async_copy(source.at[tile, :], target.at[tile, :], sems.at[which, index])
            for which, (source, target) in enumerate(((gate_hbm, gate_ref), (up_hbm, up_ref)))
        ]
        for index, tile in enumerate(tiles)
    ]
    down_copy = pltpu.make_async_copy(down_hbm, down_ref, sems.at[2, 0])
    for pair in copies:
        for copy in pair:
            copy.start()
    down_copy.start()
    x = smooth(x_ref[...], scale_ref[...])
    for pair, tile in zip(copies, tiles):
        for copy in pair:
            copy.wait()
        hidden[:, tile] = hidden_tile(x, gate_ref[tile, :], up_ref[tile, :])
    down_copy.wait()
    out_ref[...] = jnp.dot(hidden[...], down_ref[...], preferred_element_type=jnp.float32)


def arrived_kernel(x_ref, scale_ref, gate_ref, up_ref, down_ref, out_ref, hidden):
    x = smooth(x_ref[...], scale_ref[...])
    for tile in unit_tiles(gate_ref.shape[0]):
        hidden[:, tile] = hidden_tile(x, gate_ref[tile, :], up_ref[tile, :])
    out_ref[...] = jnp.dot(hidden[...], down_ref[...], preferred_element_type=jnp.float32).astype(out_ref.dtype)


def cost(rows, width, units):
    return pl.CostEstimate(flops=6 * rows * width * units, bytes_accessed=6 * units * width, transcendentals=2 * rows * units)


def own_block(x, scale, weights):
    rows, width = x.shape
    units = weights[0].shape[0]
    held = tuple(jax.ShapeDtypeStruct(w.shape, w.dtype) for w in weights)
    part, *kept = pl.pallas_call(
        own_kernel,
        out_shape=(jax.ShapeDtypeStruct((rows, width), jnp.float32),) + held,
        in_specs=[VMEM_SPEC] * 2 + [HBM_SPEC] * 3,
        out_specs=(VMEM_SPEC,) * 4,
        scratch_shapes=[pltpu.VMEM((rows, units), jnp.bfloat16), pltpu.SemaphoreType.DMA((3, len(unit_tiles(units))))],
        compiler_params=pltpu.CompilerParams(vmem_limit_bytes=OWN_VMEM_LIMIT),
        cost_estimate=cost(rows, width, units),
        name="own_block",
    )(x, scale, *weights)
    return part, kept


def arrived_block(x, scale, weights, dtype):
    rows, width = x.shape
    units = weights[0].shape[0]
    return pl.pallas_call(
        arrived_kernel,
        out_shape=jax.ShapeDtypeStruct((rows, width), dtype),
        in_specs=[VMEM_SPEC] * 5,
        out_specs=VMEM_SPEC,
        scratch_shapes=[pltpu.VMEM((rows, units), jnp.bfloat16)],
        compiler_params=pltpu.CompilerParams(vmem_limit_bytes=VMEM_LIMIT),
        cost_estimate=cost(rows, width, units),
        name="arrived_block",
    )(x, scale, *weights)


def hop(block, route, axes="tensor"):
    return lax.ppermute(block, axes, route)


def add(arrived, part):
    return (arrived.astype(jnp.float32) + part).astype(jnp.bfloat16)


def line_of_four(tokens, own, scale, weights):
    beside = [(place, place ^ 1) for place in range(4)]
    groups = range(lax.axis_size("dp"))

    def far(distances):
        return [(group * 4 + place, group * 4 + (place ^ distances[group % 2])) for group in groups for place in range(4)]

    def far_hop(block, distances):
        return hop(block, far(distances), ("dp", "tensor"))

    x_1 = hop(tokens, beside)
    x_far, own = lax.optimization_barrier((far_hop(tokens, (2, 3)), own))
    part_1 = arrived_block(x_1, scale, weights, jnp.bfloat16)
    x_last = hop(x_far, beside)
    joining = hop(arrived_block(x_far, scale, weights, jnp.bfloat16), beside)
    part_last, part_1 = lax.optimization_barrier((arrived_block(x_last, scale, weights, jnp.float32), part_1))
    from_neighbour = hop(part_1, beside)
    from_far = far_hop(add(joining, part_last), (3, 2))
    return (own + from_neighbour.astype(jnp.float32) + from_far.astype(jnp.float32)).astype(jnp.bfloat16)


def folded_ring(tokens, own, scale, weights, n):
    order = list(range(0, n, 2)) + list(range(1, n, 2))[::-1]
    route = [(order[k - 1], order[k]) for k in range(n)]
    x, summed = tokens, None
    for step in range(1, n):
        x = hop(x, route)
        part = arrived_block(x, scale, weights, jnp.bfloat16 if step == 1 else jnp.float32)
        summed = part if step == 1 else add(hop(summed, route), part)
    return add(hop(summed, route), own) if n > 1 else own.astype(jnp.bfloat16)


def shards(tokens, smooth_scale, gate_weight, up_weight, down_weight):
    n = lax.axis_size("tensor")
    scale = smooth_scale[None, :]
    own, weights = own_block(tokens, scale, (gate_weight, up_weight, down_weight))
    if n == 4:
        return line_of_four(tokens, own, scale, weights)
    return folded_ring(tokens, own, scale, weights, n)


def solution(mesh):
    return jax.shard_map(
        shards,
        mesh=mesh,
        in_specs=(
            P(("dp", "tensor"), None),
            P(),
            P("tensor", None),
            P("tensor", None),
            P("tensor", None),
        ),
        out_specs=P(("dp", "tensor"), None),
        check_vma=False,
    )
```

```python
import jax
import jax.numpy as jnp
from jax import lax
from jax.experimental import pallas as pl
from jax.experimental.pallas import tpu as pltpu
from jax.sharding import PartitionSpec as P

UNIT_TILE = 256
CONTRACT_LAST = (((1,), (1,)), ((), ()))
VMEM_LIMIT = 16 * 2**20
OWN_VMEM_LIMIT = 46 * 2**20
VMEM_SPEC = pl.BlockSpec(memory_space=pltpu.VMEM)
HBM_SPEC = pl.BlockSpec(memory_space=pltpu.HBM)


def unit_tiles(units):
    return [pl.ds(start, min(UNIT_TILE, units - start)) for start in range(0, units, UNIT_TILE)]


def hidden_tile(x, gate, up):
    gate_out = lax.dot_general(x, gate, CONTRACT_LAST, preferred_element_type=jnp.float32)
    up_out = lax.dot_general(x, up, CONTRACT_LAST, preferred_element_type=jnp.float32)
    return (gate_out / (1.0 + jnp.exp(-gate_out)) * up_out).astype(jnp.bfloat16)


def smooth(x, scale):
    return (x.astype(jnp.float32) / scale).astype(jnp.bfloat16)


def second_core():
    return lax.rem(lax.axis_index("dp"), 2) == 1


def own_kernel(x_ref, scale_ref, gate_hbm, up_hbm, down_hbm, out_ref, held_ref, gate_ref, up_ref, down_ref, hidden, sems):
    tiles = unit_tiles(gate_hbm.shape[0])
    copies = [
        [
            pltpu.make_async_copy(source.at[tile, :], target.at[tile, :], sems.at[which, index])
            for which, (source, target) in enumerate(((gate_hbm, gate_ref), (up_hbm, up_ref)))
        ]
        for index, tile in enumerate(tiles)
    ]
    down_copy = pltpu.make_async_copy(down_hbm, down_ref, sems.at[2, 0])
    for pair in copies:
        for copy in pair:
            copy.start()
    down_copy.start()
    held_ref[...] = x_ref[...]
    x = smooth(x_ref[...], scale_ref[...])
    for pair, tile in zip(copies, tiles):
        for copy in pair:
            copy.wait()

        @pl.when(jnp.logical_not(second_core()))
        def _():
            hidden[:, tile] = hidden_tile(x, gate_ref[tile, :], up_ref[tile, :])

    down_copy.wait()

    @pl.when(jnp.logical_not(second_core()))
    def _():
        out_ref[...] = jnp.dot(hidden[...], down_ref[...], preferred_element_type=jnp.float32)


def multiply(x_ref, scale_ref, gate_ref, up_ref, down_ref, out_ref, hidden):
    x = smooth(x_ref[...], scale_ref[...])
    for tile in unit_tiles(gate_ref.shape[0]):
        hidden[:, tile] = hidden_tile(x, gate_ref[tile, :], up_ref[tile, :])
    out_ref[...] = jnp.dot(hidden[...], down_ref[...], preferred_element_type=jnp.float32).astype(out_ref.dtype)


def arrived_kernel(x_ref, *refs):
    multiply(x_ref, *refs)


def arrived_and_own_kernel(x_ref, scale_ref, gate_ref, up_ref, down_ref, held_ref, own_ref, out_ref, own_out, hidden):
    weights = (scale_ref, gate_ref, up_ref, down_ref)

    @pl.when(second_core())
    def _():
        multiply(held_ref, *weights, own_out, hidden)

    @pl.when(jnp.logical_not(second_core()))
    def _():
        own_out[...] = own_ref[...]

    multiply(x_ref, *weights, out_ref, hidden)


def cost(rows, width, units):
    return pl.CostEstimate(flops=6 * rows * width * units, bytes_accessed=6 * units * width, transcendentals=2 * rows * units)


def own_block(x, scale, weights):
    rows, width = x.shape
    units = weights[0].shape[0]
    held = tuple(jax.ShapeDtypeStruct(w.shape, w.dtype) for w in weights)
    part, tokens, *kept = pl.pallas_call(
        own_kernel,
        out_shape=(jax.ShapeDtypeStruct((rows, width), jnp.float32), jax.ShapeDtypeStruct(x.shape, x.dtype)) + held,
        in_specs=[VMEM_SPEC] * 2 + [HBM_SPEC] * 3,
        out_specs=(VMEM_SPEC,) * 5,
        scratch_shapes=[pltpu.VMEM((rows, units), jnp.bfloat16), pltpu.SemaphoreType.DMA((3, len(unit_tiles(units))))],
        compiler_params=pltpu.CompilerParams(vmem_limit_bytes=OWN_VMEM_LIMIT),
        cost_estimate=cost(rows, width, units),
        name="own_block",
    )(x, scale, *weights)
    return part, tokens, kept


def arrived_block(x, scale, weights, dtype):
    rows, width = x.shape
    units = weights[0].shape[0]
    return pl.pallas_call(
        arrived_kernel,
        out_shape=jax.ShapeDtypeStruct((rows, width), dtype),
        in_specs=[VMEM_SPEC] * 5,
        out_specs=VMEM_SPEC,
        scratch_shapes=[pltpu.VMEM((rows, units), jnp.bfloat16)],
        compiler_params=pltpu.CompilerParams(vmem_limit_bytes=VMEM_LIMIT),
        cost_estimate=cost(rows, width, units),
        name="arrived_block",
    )(x, scale, *weights)


def arrived_and_own_block(x, scale, weights, dtype, held, own):
    rows, width = x.shape
    units = weights[0].shape[0]
    return pl.pallas_call(
        arrived_and_own_kernel,
        out_shape=(jax.ShapeDtypeStruct((rows, width), dtype), jax.ShapeDtypeStruct((rows, width), jnp.float32)),
        in_specs=[VMEM_SPEC] * 7,
        out_specs=(VMEM_SPEC,) * 2,
        scratch_shapes=[pltpu.VMEM((rows, units), jnp.bfloat16)],
        compiler_params=pltpu.CompilerParams(vmem_limit_bytes=VMEM_LIMIT),
        cost_estimate=cost(rows, width, units),
        name="arrived_and_own_block",
    )(x, scale, *weights, held, own)


def hop(block, route, axes="tensor"):
    return lax.ppermute(block, axes, route)


def add(arrived, part):
    return (arrived.astype(jnp.float32) + part).astype(jnp.bfloat16)


def line_of_four(tokens, held, own, scale, weights):
    beside = [(place, place ^ 1) for place in range(4)]
    groups = range(lax.axis_size("dp"))

    def far(distances):
        return [(group * 4 + place, group * 4 + (place ^ distances[group % 2])) for group in groups for place in range(4)]

    def far_hop(block, distances):
        return hop(block, far(distances), ("dp", "tensor"))

    x_1 = hop(tokens, beside)
    x_far, own = lax.optimization_barrier((far_hop(tokens, (2, 3)), own))
    x_last = hop(x_far, beside)
    part_far, own = arrived_and_own_block(x_far, scale, weights, jnp.bfloat16, held, own)
    joining = hop(part_far, beside)
    from_neighbour = hop(arrived_block(x_1, scale, weights, jnp.bfloat16), beside)
    from_far = far_hop(add(joining, arrived_block(x_last, scale, weights, jnp.float32)), (3, 2))
    return (own + from_neighbour.astype(jnp.float32) + from_far.astype(jnp.float32)).astype(jnp.bfloat16)


def folded_ring(tokens, held, own, scale, weights, n):
    order = list(range(0, n, 2)) + list(range(1, n, 2))[::-1]
    route = [(order[k - 1], order[k]) for k in range(n)]
    x, summed = tokens, None
    for step in range(1, n):
        x = hop(x, route)
        if step == 1:
            summed, own = arrived_and_own_block(x, scale, weights, jnp.bfloat16, held, own)
        else:
            summed = add(hop(summed, route), arrived_block(x, scale, weights, jnp.float32))
    return add(hop(summed, route), own)


def shards(tokens, smooth_scale, gate_weight, up_weight, down_weight):
    n = lax.axis_size("tensor")
    scale = smooth_scale[None, :]
    own, held, weights = own_block(tokens, scale, (gate_weight, up_weight, down_weight))
    if n == 4:
        return line_of_four(tokens, held, own, scale, weights)
    return folded_ring(tokens, held, own, scale, weights, n)


def solution(mesh):
    return jax.shard_map(
        shards,
        mesh=mesh,
        in_specs=(
            P(("dp", "tensor"), None),
            P(),
            P("tensor", None),
            P("tensor", None),
            P("tensor", None),
        ),
        out_specs=P(("dp", "tensor"), None),
        check_vma=False,
    )
```

```python
import jax
import jax.numpy as jnp
from jax import lax
from jax.experimental import pallas as pl
from jax.experimental.pallas import tpu as pltpu
from jax.sharding import PartitionSpec as P

UNIT_TILE = 256
CONTRACT_LAST = (((1,), (1,)), ((), ()))
VMEM_LIMIT = 16 * 2**20
OWN_VMEM_LIMIT = 46 * 2**20
VMEM_SPEC = pl.BlockSpec(memory_space=pltpu.VMEM)
HBM_SPEC = pl.BlockSpec(memory_space=pltpu.HBM)


def unit_tiles(units):
    return [pl.ds(start, min(UNIT_TILE, units - start)) for start in range(0, units, UNIT_TILE)]


def hidden_tile(x, gate, up):
    gate_out = lax.dot_general(x, gate, CONTRACT_LAST, preferred_element_type=jnp.float32)
    up_out = lax.dot_general(x, up, CONTRACT_LAST, preferred_element_type=jnp.float32)
    return (gate_out / (1.0 + jnp.exp(-gate_out)) * up_out).astype(jnp.bfloat16)


def smooth(x, scale):
    return (x.astype(jnp.float32) / scale).astype(jnp.bfloat16)


def own_kernel(x_ref, scale_ref, gate_hbm, up_hbm, down_hbm, out_ref, gate_ref, up_ref, down_ref, hidden, sems):
    tiles = unit_tiles(gate_hbm.shape[0])
    copies = [
        [
            pltpu.make_async_copy(source.at[tile, :], target.at[tile, :], sems.at[which, index])
            for which, (source, target) in enumerate(((gate_hbm, gate_ref), (up_hbm, up_ref)))
        ]
        for index, tile in enumerate(tiles)
    ]
    down_copy = pltpu.make_async_copy(down_hbm, down_ref, sems.at[2, 0])
    for pair in copies:
        for copy in pair:
            copy.start()
    down_copy.start()
    x = smooth(x_ref[...], scale_ref[...])
    for pair, tile in zip(copies, tiles):
        for copy in pair:
            copy.wait()
        hidden[:, tile] = hidden_tile(x, gate_ref[tile, :], up_ref[tile, :])
    down_copy.wait()
    out_ref[...] = jnp.dot(hidden[...], down_ref[...], preferred_element_type=jnp.float32)


def arrived_kernel(x_ref, scale_ref, gate_ref, up_ref, down_ref, out_ref, hidden):
    x = smooth(x_ref[...], scale_ref[...])
    for tile in unit_tiles(gate_ref.shape[0]):
        hidden[:, tile] = hidden_tile(x, gate_ref[tile, :], up_ref[tile, :])
    out_ref[...] = jnp.dot(hidden[...], down_ref[...], preferred_element_type=jnp.float32).astype(out_ref.dtype)


def cost(rows, width, units):
    return pl.CostEstimate(flops=6 * rows * width * units, bytes_accessed=6 * units * width, transcendentals=2 * rows * units)


def own_block(x, scale, weights):
    rows, width = x.shape
    units = weights[0].shape[0]
    held = tuple(jax.ShapeDtypeStruct(w.shape, w.dtype) for w in weights)
    part, *kept = pl.pallas_call(
        own_kernel,
        out_shape=(jax.ShapeDtypeStruct((rows, width), jnp.float32),) + held,
        in_specs=[VMEM_SPEC] * 2 + [HBM_SPEC] * 3,
        out_specs=(VMEM_SPEC,) * 4,
        scratch_shapes=[pltpu.VMEM((rows, units), jnp.bfloat16), pltpu.SemaphoreType.DMA((3, len(unit_tiles(units))))],
        compiler_params=pltpu.CompilerParams(vmem_limit_bytes=OWN_VMEM_LIMIT),
        cost_estimate=cost(rows, width, units),
        name="own_block",
    )(x, scale, *weights)
    return part, kept


def arrived_block(x, scale, weights, dtype):
    rows, width = x.shape
    units = weights[0].shape[0]
    return pl.pallas_call(
        arrived_kernel,
        out_shape=jax.ShapeDtypeStruct((rows, width), dtype),
        in_specs=[VMEM_SPEC] * 5,
        out_specs=VMEM_SPEC,
        scratch_shapes=[pltpu.VMEM((rows, units), jnp.bfloat16)],
        compiler_params=pltpu.CompilerParams(vmem_limit_bytes=VMEM_LIMIT),
        cost_estimate=cost(rows, width, units),
        name="arrived_block",
    )(x, scale, *weights)


def hop(block, route, axes="tensor"):
    return lax.ppermute(block, axes, route)


def add(arrived, part):
    return (arrived.astype(jnp.float32) + part).astype(jnp.bfloat16)


def line_of_four(tokens, own, scale, weights):
    beside = [(place, place ^ 1) for place in range(4)]
    groups = range(lax.axis_size("dp"))

    def far(distances):
        return [(group * 4 + place, group * 4 + (place ^ distances[group % 2])) for group in groups for place in range(4)]

    def far_hop(block, distances):
        return hop(block, far(distances), ("dp", "tensor"))

    x_1 = hop(tokens, beside)
    x_far, own = lax.optimization_barrier((far_hop(tokens, (2, 3)), own))
    part_1 = arrived_block(x_1, scale, weights, jnp.bfloat16)
    x_last = hop(x_far, beside)
    from_first = far_hop(arrived_block(x_far, scale, weights, jnp.bfloat16), (2, 3))
    from_neighbour = hop(part_1, beside)
    from_last = far_hop(arrived_block(x_last, scale, weights, jnp.bfloat16), (3, 2))
    for arrived in (from_first, from_neighbour, from_last):
        own = own + arrived.astype(jnp.float32)
    return own.astype(jnp.bfloat16)


def folded_ring(tokens, own, scale, weights, n):
    order = list(range(0, n, 2)) + list(range(1, n, 2))[::-1]
    route = [(order[k - 1], order[k]) for k in range(n)]
    x, summed = tokens, None
    for step in range(1, n):
        x = hop(x, route)
        part = arrived_block(x, scale, weights, jnp.bfloat16 if step == 1 else jnp.float32)
        summed = part if step == 1 else add(hop(summed, route), part)
    return add(hop(summed, route), own) if n > 1 else own.astype(jnp.bfloat16)


def shards(tokens, smooth_scale, gate_weight, up_weight, down_weight):
    n = lax.axis_size("tensor")
    scale = smooth_scale[None, :]
    own, weights = own_block(tokens, scale, (gate_weight, up_weight, down_weight))
    if n == 4:
        return line_of_four(tokens, own, scale, weights)
    return folded_ring(tokens, own, scale, weights, n)


def solution(mesh):
    return jax.shard_map(
        shards,
        mesh=mesh,
        in_specs=(
            P(("dp", "tensor"), None),
            P(),
            P("tensor", None),
            P("tensor", None),
            P("tensor", None),
        ),
        out_specs=P(("dp", "tensor"), None),
        check_vma=False,
    )
```
